32 devices in a mesh: groups: 2 (over x), train: 16 (over z, y, core).
Axes of the slice: x: 2, y: 2, z: 4, core: 2. Of those that a mesh axis runs over, the one named last changes fastest.
Arguments:
- query_grads: bfloat16 [768, 8192], P(('groups', 'train')), parts along dimension 0
- train_grads: bfloat16 [8192, 8192], P(('groups', 'train')), parts along dimension 0
- precondition: float32 [16384], P('groups'), parts along dimension 0, may hold values from 0.2 to 5
- routes: int32 [768, 4], P('groups'), parts along dimension 0, may hold values from 0 to 15, all different within a row; in each aligned block of 24 rows (0 to 23, 24 to 47, ...) at most 8 rows name the same one
- owner: int32 [32], P('groups'), parts along dimension 0, may hold values from 0 to 15, each once
- counts: int32 [32], P(('groups', 'train')), parts along dimension 0, may hold values from 32 to 256, as said below
Outputs:
- scores: float32 [768, 4, 256], P(('groups', 'train')), parts along dimension 0
The draws below stay inside these ranges and needn't reach their ends.
There are 2 independent parts, one for each index of `groups`. The reference program is written for one: setup_inputs(seed, part) draws one part's arguments, and reference() takes and returns one part's arrays. A program takes and returns all parts, laid end to end along the dimension named above; each array names one. Nothing has to cross between parts.
Inputs may be any that keep to these rules, and one draw needn't show every extreme that they name: `routes`: each row names 4 different train shards; among the 24 queries of one block no shard is named by more than 8, and in some blocks a shard is named by exactly 8; every shard is named by some query. `owner`: A permutation of the train devices. `counts`: some shard is full and some holds exactly 32 examples; the valid examples are the first ones of a shard.
All inputs are finite; a program needn't handle non-finite values.
Results may differ from the reference program's by a relative error of at most 0.003.
Values may be sent and summed in bfloat16 or wider, within the bound.
A program may use at most 128 MiB of HBM per device.

```python
import math
import jax
import jax.numpy as jnp
import numpy as np
from jax import lax

DIM = 8192
TRAIN_DEV = 256
Q_DEV = 24
CAP = 8
FANOUT = 4
QUERIES = 384
TRAIN_ROWS = 4096
N_TRAIN = 16


def rough_rows(key, row_count, columns):
    key_list = jax.random.split(key, 5)
    normal_part = jax.random.normal(key_list[0], (row_count, columns), jnp.float32)
    base = normal_part
    row_scale = jnp.exp(jax.random.uniform(key_list[3], (row_count, 1), jnp.float32, 0.0, 2.302585))
    column_scale = jnp.exp(jax.random.uniform(key_list[4], (1, columns), jnp.float32, 0.0, 2.302585))
    return base * row_scale * column_scale


def draw_query_grads(key, part):
    key = jax.random.fold_in(key, 11)
    values = rough_rows(key, QUERIES, DIM)
    return values.astype(jnp.bfloat16)


def draw_train_grads(key, part):
    key = jax.random.fold_in(key, 13)
    values = rough_rows(key, TRAIN_ROWS, DIM)
    return values.astype(jnp.bfloat16)


def draw_counts(key, part):
    key = jax.random.fold_in(key, 17)
    key_list = jax.random.split(key, 4)
    lowest = TRAIN_DEV // 8
    first_draw = jax.random.randint(key_list[0], (N_TRAIN,), lowest, TRAIN_DEV + 1, jnp.int32)
    second_draw = jax.random.randint(key_list[1], (N_TRAIN,), lowest, TRAIN_DEV + 1, jnp.int32)
    values = jnp.minimum(first_draw, second_draw)
    full_at = jax.random.randint(key_list[2], (), 0, N_TRAIN, jnp.int32)
    empty_at = (full_at + 1 + jax.random.randint(key_list[3], (), 0, N_TRAIN - 1, jnp.int32)) % N_TRAIN
    shard_ids = jnp.arange(N_TRAIN, dtype=jnp.int32)
    values = jnp.where(shard_ids == full_at, TRAIN_DEV, values)
    values = jnp.where(shard_ids == empty_at, lowest, values)
    return values.astype(jnp.int32)


def routed_block(own_key, own, number, rows, count, top, reach, skew):
    order = jax.random.permutation(own_key, count)
    packed, usual = load_shares(count, rows * top, reach, skew, True), load_shares(count, rows * top, reach, skew, False)
    places = jnp.arange(count)

    def named(tallies, rotation):
        used = int((tallies > 0).sum())
        fixed = max(1, used // 4)
        passed = fixed + (places - fixed + rotation * (used - fixed)) % max(1, count - fixed)
        return jnp.zeros((count,), jnp.int32).at[order[jnp.where(places < fixed, places, passed)]].set(jnp.asarray(tallies, jnp.int32))

    tallies = jnp.where(number % 4 == 0, named(packed, number // 4), named(usual, number - number // 4 - 1))
    mixed = jax.random.permutation(jax.random.fold_in(own, 3), count)
    donor, taker = mixed[0:count // 2 * 2:2], mixed[1:count // 2 * 2:2]
    room = jnp.minimum(tallies[donor] - 1, reach - tallies[taker]) // 2
    room = jnp.where((donor == order[0]) | (taker == order[0]) | (tallies[taker] == 0), 0, jnp.maximum(room, 0))
    passed = jax.random.randint(jax.random.fold_in(own, 4), (count // 2,), 0, 1 << 20) % (room + 1)
    tallies = tallies.at[donor].add(-passed).at[taker].add(passed)
    items = jnp.searchsorted(jnp.cumsum(tallies), jnp.arange(rows * top), side="right").astype(jnp.int32)
    grid = items.reshape(top, rows).T
    grid = grid[jax.random.permutation(jax.random.fold_in(own, 1), rows)]
    rotation = jax.random.randint(jax.random.fold_in(own, 2), (rows, 1), 0, top)
    return jnp.take_along_axis(grid, (jnp.arange(top)[None, :] + rotation) % top, axis=1)


def load_shares(number_of, total, limit, slope, full):
    portions = [(1 << 20) // math.isqrt(standing ** slope) + 1 for standing in range(1, number_of + 1)]
    largest = limit if full else min(limit, max(-(-total // number_of), total * portions[0] // sum(portions)))
    least = 1 if total - largest >= number_of - 1 else 0
    holding, spare = [largest] + [least] * (number_of - 1), total - largest - least * (number_of - 1)
    while spare > 0:
        free = [i for i in range(1, number_of) if holding[i] < largest] or [i for i in range(1, number_of) if holding[i] < limit]
        whole, remaining = sum([portions[i] for i in free]), spare
        for i in free:
            addition = min(limit - holding[i], max(1, remaining * portions[i] // whole), spare)
            holding[i] = holding[i] + addition
            spare = spare - addition
    return np.array(holding)


def setup_inputs(seed: int = 0, part: int = 0) -> dict:
    streams_of = jax.random.split(jax.random.key(seed), 7)
    own_keys = jax.random.split(jax.random.fold_in(streams_of[6], part), 7)
    query_grads = draw_query_grads(jax.random.fold_in(jax.random.fold_in(streams_of[6], part), 71), part)
    train_grads = draw_train_grads(jax.random.fold_in(jax.random.fold_in(streams_of[6], part), 71), part)
    precondition = jnp.clip(jnp.exp(jax.random.uniform(own_keys[2], (DIM,), jnp.float32, math.log(0.2), math.log(5.0))), 0.2, 5.0)
    routes_keys = jax.random.split(jax.random.fold_in(own_keys[3], 1), QUERIES // Q_DEV)
    routes_turns = jax.random.permutation(jax.random.fold_in(own_keys[3], 3), QUERIES // Q_DEV)
    routes = jax.vmap(lambda own, number: routed_block(jax.random.fold_in(own_keys[3], 2), own, number, Q_DEV, N_TRAIN, FANOUT, CAP, 2))(routes_keys, routes_turns).reshape((QUERIES, FANOUT))
    owner = jax.random.permutation(own_keys[4], N_TRAIN).astype(jnp.int32)
    counts = draw_counts(jax.random.fold_in(jax.random.fold_in(streams_of[6], part), 71), part)
    return dict(query_grads=query_grads, train_grads=train_grads, precondition=precondition, routes=routes, owner=owner, counts=counts)


def normalize(query_grads, precondition):
    scaled = query_grads.astype(jnp.float32) * precondition[None, :]
    spread = jnp.sqrt(lax.optimization_barrier(jnp.mean(scaled * scaled, axis=1, keepdims=True)) + 1e-06)
    return (scaled / spread).astype(jnp.bfloat16)

def reference(query_grads, train_grads, precondition, routes, owner, counts):
    normed = normalize(query_grads, precondition)
    blocks = routes.reshape(N_TRAIN, Q_DEV, FANOUT)

    def one_shard(shard, gathered):
        match = blocks == shard
        named = jnp.any(match, axis=2)
        named_int = named.astype(jnp.int32)
        column = lax.optimization_barrier(jnp.sum(match.astype(jnp.int32) * jnp.arange(FANOUT, dtype=jnp.int32)[None, None, :], axis=2, dtype=jnp.int32))
        order = jnp.cumsum(named_int, axis=1, dtype=jnp.int32) - named_int
        chosen = named[:, :, None] & (order[:, :, None] == jnp.arange(CAP, dtype=jnp.int32)[None, None, :])
        filled = jnp.any(chosen, axis=1).reshape(-1)
        member = lax.optimization_barrier(jnp.sum(chosen.astype(jnp.int32) * jnp.arange(Q_DEV, dtype=jnp.int32)[None, :, None], axis=1, dtype=jnp.int32))
        query_ids = (jnp.arange(N_TRAIN, dtype=jnp.int32)[:, None] * Q_DEV + member).reshape(-1)
        slot_column = jnp.take_along_axis(column, member, axis=1).reshape(-1)
        rows = jnp.where(filled[:, None], normed[query_ids], jnp.zeros((), jnp.bfloat16))
        slab = lax.dynamic_slice_in_dim(train_grads, shard * TRAIN_DEV, TRAIN_DEV, 0)
        row_norm = jnp.sqrt(lax.optimization_barrier(jnp.mean(jnp.square(slab.astype(jnp.float32)), axis=1)) + 1e-06)
        dotted = jnp.dot(rows, slab.T, preferred_element_type=jnp.float32)
        live = jnp.arange(TRAIN_DEV, dtype=jnp.int32) < counts[shard]
        tiles = jnp.where(live[None, :], dotted / (row_norm[None, :] * math.sqrt(DIM)), 0.0)
        flat_index = jnp.where(filled, query_ids * FANOUT + slot_column, QUERIES * FANOUT)
        return gathered.at[flat_index].set(tiles, mode='drop')
    start = jnp.zeros((QUERIES * FANOUT, TRAIN_DEV), jnp.float32)
    gathered = lax.fori_loop(0, N_TRAIN, one_shard, start)
    by_block = gathered.reshape(N_TRAIN, Q_DEV, FANOUT, TRAIN_DEV)
    placed = jnp.zeros_like(by_block).at[owner].set(by_block)
    return placed.reshape(QUERIES, FANOUT, TRAIN_DEV)
```

```python
import math

import jax
import jax.numpy as jnp
from jax import lax
from jax.experimental import pallas as pl
from jax.experimental.pallas import tpu as pltpu
from jax.sharding import PartitionSpec as P

CAP = 8


def normalize(query_grads, precondition):
    scaled = query_grads.astype(jnp.float32) * precondition[None, :]
    spread = jnp.sqrt(jnp.mean(scaled * scaled, axis=1, keepdims=True) + 1e-06)
    return (scaled / spread).astype(jnp.bfloat16)


def slot_table(block_routes, shards):
    hit_table = jnp.sum(
        (block_routes[:, :, None] == jnp.arange(shards, dtype=jnp.int32)[None, None, :]).astype(
            jnp.int32
        ),
        axis=1,
        dtype=jnp.int32,
    )
    earlier = jnp.cumsum(hit_table, axis=0, dtype=jnp.int32) - hit_table
    return jnp.take_along_axis(earlier, block_routes, axis=1)


def fetch_home(result):
    return lax.all_to_all(result, "train", split_axis=0, concat_axis=0, tiled=True)


def per_device(query_grads, train_grads, precondition, routes, owner, counts):
    shards = lax.axis_size("train")
    position = lax.axis_index("train")
    block_size = query_grads.shape[0]
    features = train_grads.shape[1]
    capacity = CAP
    normed = normalize(query_grads, precondition)
    own_routes = lax.dynamic_slice_in_dim(routes, position * block_size, block_size, 0)
    target = own_routes * capacity + slot_table(own_routes, shards)
    lane_ids = jnp.arange(shards * capacity, dtype=jnp.int32)
    picked = jnp.any(target[:, :, None] == lane_ids[None, None, :], axis=1).astype(jnp.bfloat16)
    outgoing = lax.dot_general(
        picked, normed, (((0,), (0,)), ((), ())), preferred_element_type=jnp.float32
    )
    outgoing = outgoing.astype(jnp.bfloat16).reshape(shards, capacity, features)
    inverse = jnp.zeros((shards,), jnp.int32).at[owner].set(jnp.arange(shards, dtype=jnp.int32))
    row_norm = jnp.sqrt(jnp.mean(jnp.square(train_grads.astype(jnp.float32)), axis=1) + 1e-06)
    filled = jnp.arange(train_grads.shape[0], dtype=jnp.int32) < counts[0]
    arrived = lax.all_to_all(outgoing, "train", split_axis=0, concat_axis=0, tiled=True)
    flattened = arrived.reshape(-1, features)
    dotted = lax.dot_general(
        flattened, train_grads, (((1,), (1,)), ((), ())), preferred_element_type=jnp.float32
    )
    result = jnp.where(filled[None, :], dotted / (row_norm[None, :] * math.sqrt(features)), 0.0)
    result = result.reshape(arrived.shape[0], arrived.shape[1], -1)
    returned = fetch_home(result[inverse])
    owned_block = inverse[position]
    their_routes = lax.dynamic_slice_in_dim(routes, owned_block * block_size, block_size, 0)
    pickup = their_routes * capacity + slot_table(their_routes, shards)
    return returned.reshape(shards * capacity, -1)[pickup]


LINE = 4
PARTS = 4


def grid_kernel(routes_pairs, routes_flat, owner, counts, query, scale, train, out,
                other, held, train_vmem, scaled, picked, select, results, outgoing, incoming,
                raw_sem, train_sem, z_send, z_recv, y_send, y_recv, c_send, c_recv, s_send, s_recv):
    rows, features = query.shape
    pair = 2 * rows
    total = held.shape[2]
    extra = total - pair
    width = held.shape[3]
    columns = train_vmem.shape[0]
    shards = 4 * LINE
    me = lax.axis_index("train")
    core = me % 2
    side = (me // 2) % 2
    place = me // 4
    mate = place * 4 + side * 2 + (1 - core)
    across = place * 4 + (1 - side) * 2 + core
    after, before = me + 4, me - 4

    barrier = pltpu.get_barrier_semaphore()
    for hop in range(1, shards):
        pl.semaphore_signal(barrier, inc=1, device_id={"train": (me + hop) % shards},
                            device_id_type=pl.DeviceIdType.MESH)
    load = pltpu.make_async_copy(train, train_vmem, train_sem)
    load.start()

    def remote(source, target, send, recv, device):
        return pltpu.make_async_remote_copy(
            src_ref=source, dst_ref=target, send_sem=send, recv_sem=recv,
            device_id={"train": device}, device_id_type=pl.DeviceIdType.MESH)

    def z_copy(direction, step, origin, part, device):
        block = held.at[origin, core * PARTS + part, pl.ds(0, pair)]
        return remote(block, block, z_send.at[direction, step, part], z_recv.at[origin, part], device)

    def y_copy(origin, part):
        block = held.at[origin, core * PARTS + part, pl.ds(pair, extra)]
        return remote(picked.at[origin, part], block, y_send.at[origin, part], y_recv.at[origin, part], across)

    def c_copy(kind, origin, part, lane):
        span = pl.ds(0, pair) if kind == 0 else pl.ds(pair, extra)
        block = held.at[origin, lane * PARTS + part, span]
        return remote(block, block, c_send.at[kind, origin, part], c_recv.at[kind, origin, part], mate)

    def slots(pairs, shard):
        hit = jnp.sum((pairs == shard).astype(jnp.float32), axis=0, keepdims=True)
        first = lax.broadcasted_iota(jnp.int32, (pair, pair), 0)
        second = lax.broadcasted_iota(jnp.int32, (pair, pair), 1)
        earlier = ((first // rows == second // rows) & (first < second)).astype(jnp.float32)
        order = jnp.dot(jnp.broadcast_to(hit, (8, pair)), earlier, preferred_element_type=jnp.float32)[:1]
        return hit, order.astype(jnp.int32)

    def spread(block):
        def body(i, total_square):
            at = pl.ds(pl.multiple_of(i * width, width), width)
            value = block[:, at].astype(jnp.float32) * scale[:, at]
            return total_square + jnp.sum(value * value, axis=1, keepdims=True)
        square = lax.fori_loop(0, features // width, body, jnp.zeros((rows, 1), jnp.float32))
        return jnp.sqrt(square / features + 1e-06)

    for origin in range(LINE):
        pairs = routes_pairs[origin * 2 + side]
        tables = []
        for core_there in range(2):
            hit, order = slots(pairs, place * 4 + (1 - side) * 2 + core_there)
            tables.append((hit, order))
        line = lax.broadcasted_iota(jnp.int32, (extra, pair), 0)
        lane = lax.broadcasted_iota(jnp.int32, (extra, pair), 1)
        second_core = (line // CAP) % 2 == 1
        hit = jnp.where(second_core, tables[1][0], tables[0][0])
        order = jnp.where(second_core, tables[1][1], tables[0][1])
        chosen = (hit > 0.5) & (order == line % CAP) & (line // (2 * CAP) == lane // rows)
        select[origin] = chosen.astype(jnp.float32).astype(jnp.bfloat16)

    my_spread = spread(query)
    pl.semaphore_wait(barrier, shards - 1)
    swap = remote(query, other, raw_sem.at[0], raw_sem.at[1], mate)
    swap.start()
    swap.wait_recv()
    their_spread = spread(other)
    spread_first = jnp.where(core == 0, my_spread, their_spread)
    spread_second = jnp.where(core == 0, their_spread, my_spread)

    def cross(origin, part):
        block = held[origin, core * PARTS + part, pl.ds(0, pair), :]
        chosen = jnp.dot(select[origin], block, preferred_element_type=jnp.float32)
        picked[origin, part] = chosen.astype(jnp.bfloat16)
        y_copy(origin, part).start()

    def first(part, carry):
        at = pl.ds(pl.multiple_of((core * PARTS + part) * width, width), width)
        mine = query[:, at].astype(jnp.float32) * scale[:, at]
        theirs = other[:, at].astype(jnp.float32) * scale[:, at]
        top = jnp.where(core == 0, mine, theirs) / spread_first
        low = jnp.where(core == 0, theirs, mine) / spread_second
        held[place, core * PARTS + part, pl.ds(0, pair), :] = jnp.concatenate([top, low], axis=0).astype(jnp.bfloat16)

        @pl.when(place < LINE - 1)
        def _():
            z_copy(0, 0, place, part, after).start()

        @pl.when(place > 0)
        def _():
            z_copy(1, 0, place, part, before).start()

        c_copy(0, place, part, core).start()
        cross(place, part)
        return carry

    lax.fori_loop(0, PARTS, first, 0)

    def sources(step):
        if step == 0:
            return [(None, place, None)]
        return [(place >= step, place - step, 0), (place + step < LINE, place + step, 1)]

    def under(condition, body):
        if condition is None:
            body()
        else:
            pl.when(condition)(body)

    def arrive(step, part):
        for condition, origin, direction in sources(step):
            def body(origin=origin, direction=direction):
                z_copy(direction, 0, origin, part, mate).wait_recv()
                if step < LINE - 1:
                    if direction == 0:
                        @pl.when(place < LINE - 1)
                        def _():
                            z_copy(0, step, origin, part, after).start()
                    else:
                        @pl.when(place > 0)
                        def _():
                            z_copy(1, step, origin, part, before).start()
                c_copy(0, origin, part, core).start()
                cross(origin, part)
            under(condition, body)

    def crossed(step, part):
        for condition, origin, _ in sources(step):
            def body(origin=origin):
                y_copy(origin, part).wait_recv()
                c_copy(1, origin, part, core).start()
            under(condition, body)

    def multiply(step, part):
        for condition, origin, _ in sources(step):
            def body(origin=origin):
                c_copy(0, origin, part, 1 - core).wait_recv()
                c_copy(1, origin, part, 1 - core).wait_recv()
                partial = jnp.zeros((total, columns), jnp.float32)
                for lane in range(2):
                    at = pl.ds(pl.multiple_of((lane * PARTS + part) * width, width), width)
                    partial = partial + lax.dot_general(
                        held[origin, lane * PARTS + part], train_vmem[:, at], (((1,), (1,)), ((), ())),
                        preferred_element_type=jnp.float32)
                results[origin] += partial
            under(condition, body)

    def loop(*work):
        def body(part, carry):
            for call, step in work:
                call(step, part)
            return carry
        lax.fori_loop(0, PARTS, body, 0)

    results[...] = jnp.zeros_like(results)
    load.wait()

    def square(i, sums):
        at = pl.ds(pl.multiple_of(i * 128, 128), 128)
        value = train_vmem[:, at].astype(jnp.float32)
        return sums + value * value

    sums = lax.fori_loop(0, features // 128, square, jnp.zeros((columns, 128), jnp.float32))
    sums = jnp.sum(jnp.transpose(sums), axis=0, keepdims=True)
    norm = jnp.sqrt(sums / features + 1e-06) * math.sqrt(features)
    live = lax.broadcasted_iota(jnp.int32, (1, columns), 1) < counts[0]
    scaled[...] = norm

    loop((arrive, 1), (crossed, 0))
    loop((multiply, 0))
    loop((arrive, 2), (crossed, 1))
    loop((multiply, 1))

    flat = jnp.zeros((1, routes_flat.shape[1]), jnp.int32)
    for block in range(shards):
        flat = flat + jnp.where(owner[block] == me, routes_flat[block:block + 1, :], 0)
    lanes = flat.shape[1]
    fan = routes_pairs.shape[1]
    wide = jnp.broadcast_to(flat.astype(jnp.float32), (lanes, lanes))
    same = jnp.transpose(wide) == wide
    first_lane = lax.broadcasted_iota(jnp.int32, (lanes, lanes), 0) // fan
    second_lane = lax.broadcasted_iota(jnp.int32, (lanes, lanes), 1) // fan
    order = jnp.sum((same & (first_lane < second_lane)).astype(jnp.int32), axis=0, keepdims=True)
    goal = flat * CAP + order
    pickup = (lax.broadcasted_iota(jnp.int32, (shards * CAP, lanes), 0) == goal).astype(jnp.float32)
    pickup = jnp.transpose(pickup)

    loop((arrive, 3), (crossed, 2))
    loop((multiply, 2))
    loop((crossed, 3), (multiply, 3))

    gathered = jnp.zeros((shards * CAP, columns), jnp.float32)
    for origin in range(LINE):
        hit, order = slots(routes_pairs[origin * 2 + side], me)
        line = lax.broadcasted_iota(jnp.int32, (shards * CAP, pair), 0)
        lane = lax.broadcasted_iota(jnp.int32, (shards * CAP, pair), 1)
        near = (origin * 2 + side) * 2
        home = jnp.where(lane < rows, owner[near], owner[near + 1])
        chosen = ((hit > 0.5) & (order == line % CAP) & (home == line // CAP)).astype(jnp.float32)
        gathered = gathered + jnp.dot(chosen, results[origin, :pair], precision=lax.Precision.HIGHEST,
                                      preferred_element_type=jnp.float32)
        line = lax.broadcasted_iota(jnp.int32, (shards * CAP, extra), 0)
        lane = lax.broadcasted_iota(jnp.int32, (shards * CAP, extra), 1)
        far = (origin * 2 + 1 - side) * 2
        home = jnp.where(lane < 2 * CAP, owner[far], owner[far + 1])
        chosen = ((lane // CAP) % 2 == core) & (lane % CAP == line % CAP) & (home == line // CAP)
        gathered = gathered + jnp.dot(chosen.astype(jnp.float32), results[origin, pair:],
                                      precision=lax.Precision.HIGHEST, preferred_element_type=jnp.float32)
    gathered = jnp.where(live, gathered / scaled[...], 0.0)
    outgoing[...] = gathered.reshape(shards, CAP, columns)
    incoming[me] = outgoing[me]

    def score_copy(hop, peer):
        return remote(outgoing.at[peer], incoming.at[me], s_send.at[hop], s_recv.at[hop], peer)

    def send(hop, carry):
        score_copy(hop, (me + hop) % shards).start()
        return carry

    lax.fori_loop(1, shards, send, 0)

    def receive(hop, carry):
        source = (me + shards - hop) % shards
        remote(outgoing.at[source], incoming.at[source], s_send.at[hop], s_recv.at[hop], source).wait_recv()
        return carry

    lax.fori_loop(1, shards, receive, 0)
    out[...] = jnp.dot(pickup, incoming[...].reshape(shards * CAP, columns),
                       precision=lax.Precision.HIGHEST, preferred_element_type=jnp.float32)

    swap.wait_send()

    def finish(part, carry):
        for origin in range(LINE):
            y_copy(origin, part).wait_send()
            for kind in range(2):
                c_copy(kind, origin, part, core).wait_send()
        for step in range(LINE - 1):
            @pl.when((place >= step) & (place < LINE - 1))
            def _():
                z_copy(0, step, place - step, part, after).wait_send()

            @pl.when((place + step < LINE) & (place > 0))
            def _():
                z_copy(1, step, place + step, part, before).wait_send()
        return carry

    lax.fori_loop(0, PARTS, finish, 0)

    def sent(hop, carry):
        score_copy(hop, (me + hop) % shards).wait_send()
        return carry

    lax.fori_loop(1, shards, sent, 0)


def on_grid(query_grads, train_grads, precondition, routes, owner, counts):
    rows, features = query_grads.shape
    columns = train_grads.shape[0]
    fan = routes.shape[1]
    shards = 4 * LINE
    pair, extra = 2 * rows, 4 * CAP
    width = features // (2 * PARTS)
    routes_pairs = jnp.transpose(routes.reshape(2 * LINE, pair, fan), (0, 2, 1))
    routes_flat = routes.reshape(shards, rows * fan)
    vmem = pl.BlockSpec(memory_space=pltpu.VMEM)
    smem = pl.BlockSpec(memory_space=pltpu.SMEM)
    dma = pltpu.SemaphoreType.DMA
    out = pl.pallas_call(
        grid_kernel,
        out_shape=jax.ShapeDtypeStruct((rows * fan, columns), jnp.float32),
        in_specs=[vmem, vmem, smem, smem, vmem, vmem, pl.BlockSpec(memory_space=pl.ANY)],
        out_specs=vmem,
        scratch_shapes=[
            pltpu.VMEM((rows, features), jnp.bfloat16),
            pltpu.VMEM((LINE, 2 * PARTS, pair + extra, width), jnp.bfloat16),
            pltpu.VMEM((columns, features), jnp.bfloat16),
            pltpu.VMEM((1, columns), jnp.float32),
            pltpu.VMEM((LINE, PARTS, extra, width), jnp.bfloat16),
            pltpu.VMEM((LINE, extra, pair), jnp.bfloat16),
            pltpu.VMEM((LINE, pair + extra, columns), jnp.float32),
            pltpu.VMEM((shards, CAP, columns), jnp.float32),
            pltpu.VMEM((shards, CAP, columns), jnp.float32),
            dma((2,)),
            dma,
            dma((2, LINE - 1, PARTS)),
            dma((LINE, PARTS)),
            dma((LINE, PARTS)),
            dma((LINE, PARTS)),
            dma((2, LINE, PARTS)),
            dma((2, LINE, PARTS)),
            dma((shards,)),
            dma((shards,)),
        ],
        compiler_params=pltpu.CompilerParams(
            collective_id=0, has_side_effects=True, vmem_limit_bytes=40 * 1024 * 1024),
    )(routes_pairs, routes_flat, owner, counts, query_grads, precondition.reshape(1, features), train_grads)
    return out.reshape(rows, fan, columns)


def solution(mesh):
    per_part = on_grid if mesh.shape["train"] == 4 * LINE else per_device
    return jax.shard_map(
        per_part,
        mesh=mesh,
        in_specs=(
            P(("groups", "train"), None),
            P(("groups", "train"), None),
            P("groups"),
            P("groups", None),
            P("groups"),
            P(("groups", "train")),
        ),
        out_specs=P(("groups", "train"), None, None),
        check_vma=False,
    )
```

```python
import math

import jax
import jax.numpy as jnp
from jax import lax
from jax.experimental import pallas as pl
from jax.experimental.pallas import tpu as pltpu
from jax.sharding import PartitionSpec as P

CAP = 8


def normalize(query_grads, precondition):
    scaled = query_grads.astype(jnp.float32) * precondition[None, :]
    spread = jnp.sqrt(jnp.mean(scaled * scaled, axis=1, keepdims=True) + 1e-06)
    return (scaled / spread).astype(jnp.bfloat16)


def slot_table(block_routes, shards):
    hit_table = jnp.sum(
        (block_routes[:, :, None] == jnp.arange(shards, dtype=jnp.int32)[None, None, :]).astype(
            jnp.int32
        ),
        axis=1,
        dtype=jnp.int32,
    )
    earlier = jnp.cumsum(hit_table, axis=0, dtype=jnp.int32) - hit_table
    return jnp.take_along_axis(earlier, block_routes, axis=1)


def fetch_home(result):
    return lax.all_to_all(result, "train", split_axis=0, concat_axis=0, tiled=True)


def per_device(query_grads, train_grads, precondition, routes, owner, counts):
    shards = lax.axis_size("train")
    position = lax.axis_index("train")
    block_size = query_grads.shape[0]
    features = train_grads.shape[1]
    capacity = CAP
    normed = normalize(query_grads, precondition)
    own_routes = lax.dynamic_slice_in_dim(routes, position * block_size, block_size, 0)
    target = own_routes * capacity + slot_table(own_routes, shards)
    lane_ids = jnp.arange(shards * capacity, dtype=jnp.int32)
    picked = jnp.any(target[:, :, None] == lane_ids[None, None, :], axis=1).astype(jnp.bfloat16)
    outgoing = lax.dot_general(
        picked, normed, (((0,), (0,)), ((), ())), preferred_element_type=jnp.float32
    )
    outgoing = outgoing.astype(jnp.bfloat16).reshape(shards, capacity, features)
    inverse = jnp.zeros((shards,), jnp.int32).at[owner].set(jnp.arange(shards, dtype=jnp.int32))
    row_norm = jnp.sqrt(jnp.mean(jnp.square(train_grads.astype(jnp.float32)), axis=1) + 1e-06)
    filled = jnp.arange(train_grads.shape[0], dtype=jnp.int32) < counts[0]
    arrived = lax.all_to_all(outgoing, "train", split_axis=0, concat_axis=0, tiled=True)
    flattened = arrived.reshape(-1, features)
    dotted = lax.dot_general(
        flattened, train_grads, (((1,), (1,)), ((), ())), preferred_element_type=jnp.float32
    )
    result = jnp.where(filled[None, :], dotted / (row_norm[None, :] * math.sqrt(features)), 0.0)
    result = result.reshape(arrived.shape[0], arrived.shape[1], -1)
    returned = fetch_home(result[inverse])
    owned_block = inverse[position]
    their_routes = lax.dynamic_slice_in_dim(routes, owned_block * block_size, block_size, 0)
    pickup = their_routes * capacity + slot_table(their_routes, shards)
    return returned.reshape(shards * capacity, -1)[pickup]


LINE = 4
PARTS = 4


def grid_kernel(routes_any, owner_any, counts_any, query_any, scale_any, train, out,
                routes, owner, counts, query, scale_tiles, scale, pairs_held,
                mine, other, held, train_vmem, norm, picked, select, near_table, far_table,
                results, collected, outgoing, incoming,
                raw_sem, load_sem, z_send, z_recv, y_send, y_recv, c_send, c_recv, s_send, s_recv):
    rows, features = query.shape
    fan = routes.shape[0]
    half = features // 2
    pair = 2 * rows
    total = held.shape[2]
    extra = total - pair
    width = held.shape[3]
    columns = train_vmem.shape[0]
    shards = 4 * LINE
    me = lax.axis_index("train")
    core = me % 2
    side = (me // 2) % 2
    place = me // 4
    mate = place * 4 + side * 2 + (1 - core)
    across = place * 4 + (1 - side) * 2 + core
    after, before = me + 4, me - 4

    loads = [pltpu.make_async_copy(source, target, load_sem.at[i]) for i, (source, target) in enumerate(
        [(query_any, query), (scale_any, scale_tiles), (routes_any, routes),
         (owner_any, owner), (counts_any, counts), (train, train_vmem)])]
    for load in loads:
        load.start()
    barrier = pltpu.get_barrier_semaphore()
    for hop in range(1, shards):
        pl.semaphore_signal(barrier, inc=1, device_id={"train": (me + hop) % shards},
                            device_id_type=pl.DeviceIdType.MESH)

    def remote(source, target, send, recv, device):
        return pltpu.make_async_remote_copy(
            src_ref=source, dst_ref=target, send_sem=send, recv_sem=recv,
            device_id={"train": device}, device_id_type=pl.DeviceIdType.MESH)

    def z_copy(direction, step, origin, part, device):
        block = held.at[origin, core * PARTS + part, pl.ds(0, pair)]
        return remote(block, block, z_send.at[direction, step, part], z_recv.at[origin, part], device)

    def y_copy(origin, part):
        block = held.at[origin, core * PARTS + part, pl.ds(pair, extra)]
        return remote(picked.at[origin, part], block, y_send.at[origin, part], y_recv.at[origin, part], across)

    def c_copy(kind, origin, part, lane):
        span = pl.ds(0, pair) if kind == 0 else pl.ds(pair, extra)
        block = held.at[origin, lane * PARTS + part, span]
        return remote(block, block, c_send.at[kind, origin, part], c_recv.at[kind, origin, part], mate)

    def slots(pairs, shard):
        hit = jnp.sum((pairs == shard).astype(jnp.float32), axis=0, keepdims=True)
        first = lax.broadcasted_iota(jnp.int32, (pair, pair), 0)
        second = lax.broadcasted_iota(jnp.int32, (pair, pair), 1)
        earlier = ((first // rows == second // rows) & (first < second)).astype(jnp.float32)
        order = jnp.dot(jnp.broadcast_to(hit, (8, pair)), earlier, preferred_element_type=jnp.float32)[:1]
        return hit, order.astype(jnp.int32)

    for load in loads[:2]:
        load.wait()
    for i in range(features // 128):
        scale[:, pl.ds(i * 128, 128)] = scale_tiles[i:i + 1, :]

    def squares(i, total_square):
        at = pl.ds(pl.multiple_of(i * width, width), width)
        value = query[:, at].astype(jnp.float32) * scale[:, at]
        return total_square + jnp.sum(value * value, axis=1, keepdims=True)

    square = lax.fori_loop(0, 2 * PARTS, squares, jnp.zeros((rows, 1), jnp.float32))
    spread = jnp.sqrt(square / features + 1e-06)

    def normalize_part(part, carry):
        for lane in range(2):
            at = pl.ds(pl.multiple_of(lane * half + part * width, width), width)
            value = query[:, at].astype(jnp.float32) * scale[:, at]
            mine[lane, part] = (value / spread).astype(jnp.bfloat16)
        return carry

    lax.fori_loop(0, PARTS, normalize_part, 0)
    pl.semaphore_wait(barrier, shards - 1)
    swap = remote(mine.at[1 - core], other, raw_sem.at[0], raw_sem.at[1], mate)
    swap.start()

    for load in loads[2:5]:
        load.wait()
    for i in range(2 * LINE):
        pairs_held[i] = routes[:, i * pair:(i + 1) * pair]
    for origin in range(LINE):
        pairs = pairs_held[origin * 2 + side]
        tables = []
        for core_there in range(2):
            hit, order = slots(pairs, place * 4 + (1 - side) * 2 + core_there)
            tables.append((hit, order))
        line = lax.broadcasted_iota(jnp.int32, (extra, pair), 0)
        lane = lax.broadcasted_iota(jnp.int32, (extra, pair), 1)
        second_core = (line // CAP) % 2 == 1
        hit = jnp.where(second_core, tables[1][0], tables[0][0])
        order = jnp.where(second_core, tables[1][1], tables[0][1])
        chosen = (hit > 0.5) & (order == line % CAP) & (line // (2 * CAP) == lane // rows)
        select[origin] = chosen.astype(jnp.float32).astype(jnp.bfloat16)
    swap.wait_recv()

    def cross(origin, part):
        block = held[origin, core * PARTS + part, pl.ds(0, pair), :]
        chosen = jnp.dot(select[origin], block, preferred_element_type=jnp.float32)
        picked[origin, part] = chosen.astype(jnp.bfloat16)
        y_copy(origin, part).start()

    def first(part, carry):
        ours = mine[core, part].astype(jnp.float32)
        theirs = other[part].astype(jnp.float32)
        top = jnp.where(core == 0, ours, theirs)
        low = jnp.where(core == 0, theirs, ours)
        held[place, core * PARTS + part, pl.ds(0, pair), :] = jnp.concatenate([top, low], axis=0).astype(jnp.bfloat16)

        @pl.when(place < LINE - 1)
        def _():
            z_copy(0, 0, place, part, after).start()

        @pl.when(place > 0)
        def _():
            z_copy(1, 0, place, part, before).start()

        c_copy(0, place, part, core).start()
        cross(place, part)
        return carry

    lax.fori_loop(0, PARTS, first, 0)

    def sources(step):
        if step == 0:
            return [(None, place, None)]
        return [(place >= step, place - step, 0), (place + step < LINE, place + step, 1)]

    def under(condition, body):
        if condition is None:
            body()
        else:
            pl.when(condition)(body)

    def arrive(step, part):
        for condition, origin, direction in sources(step):
            def body(origin=origin, direction=direction):
                z_copy(direction, 0, origin, part, mate).wait_recv()
                if step < LINE - 1:
                    if direction == 0:
                        @pl.when(place < LINE - 1)
                        def _():
                            z_copy(0, step, origin, part, after).start()
                    else:
                        @pl.when(place > 0)
                        def _():
                            z_copy(1, step, origin, part, before).start()
                c_copy(0, origin, part, core).start()
                cross(origin, part)
            under(condition, body)

    def crossed(step, part):
        for condition, origin, _ in sources(step):
            def body(origin=origin):
                y_copy(origin, part).wait_recv()
                c_copy(1, origin, part, core).start()
            under(condition, body)

    def multiply(step, part):
        for condition, origin, _ in sources(step):
            def body(origin=origin):
                c_copy(0, origin, part, 1 - core).wait_recv()
                c_copy(1, origin, part, 1 - core).wait_recv()
                partial = jnp.zeros((total, columns), jnp.float32)
                for lane in range(2):
                    at = pl.ds(pl.multiple_of((lane * PARTS + part) * width, width), width)
                    partial = partial + lax.dot_general(
                        held[origin, lane * PARTS + part], train_vmem[:, at], (((1,), (1,)), ((), ())),
                        preferred_element_type=jnp.float32)
                results[origin] += partial
            under(condition, body)

    def loop(*work):
        def body(part, carry):
            for call, step in work:
                call(step, part)
            return carry
        lax.fori_loop(0, PARTS, body, 0)

    def collect(step):
        for condition, origin, _ in sources(step):
            def body(origin=origin):
                collected[...] += jnp.dot(
                    near_table[origin], results[origin, pl.ds(0, pair), :],
                    precision=lax.Precision.HIGHEST, preferred_element_type=jnp.float32)
                collected[...] += jnp.dot(
                    far_table[origin], results[origin, pl.ds(pair, extra), :],
                    precision=lax.Precision.HIGHEST, preferred_element_type=jnp.float32)
            under(condition, body)

    results[...] = jnp.zeros_like(results)
    collected[...] = jnp.zeros_like(collected)

    for origin in range(LINE):
        hit, order = slots(pairs_held[origin * 2 + side], me)
        line = lax.broadcasted_iota(jnp.int32, (shards * CAP, pair), 0)
        lane = lax.broadcasted_iota(jnp.int32, (shards * CAP, pair), 1)
        near = (origin * 2 + side) * 2
        home = jnp.where(lane < rows, owner[near], owner[near + 1])
        chosen = (hit > 0.5) & (order == line % CAP) & (home == line // CAP)
        near_table[origin] = chosen.astype(jnp.float32)
        line = lax.broadcasted_iota(jnp.int32, (shards * CAP, extra), 0)
        lane = lax.broadcasted_iota(jnp.int32, (shards * CAP, extra), 1)
        far = (origin * 2 + 1 - side) * 2
        home = jnp.where(lane < 2 * CAP, owner[far], owner[far + 1])
        chosen = ((lane // CAP) % 2 == core) & (lane % CAP == line % CAP) & (home == line // CAP)
        far_table[origin] = chosen.astype(jnp.float32)

    loop((arrive, 1), (crossed, 0))
    loads[5].wait()

    def train_squares(i, sums):
        at = pl.ds(pl.multiple_of(i * 512, 512), 512)
        value = train_vmem[:, at].astype(jnp.float32)
        value = value * value
        return sums + (value[:, :128] + value[:, 128:256]) + (value[:, 256:384] + value[:, 384:])

    sums = lax.fori_loop(0, features // 512, train_squares, jnp.zeros((columns, 128), jnp.float32))
    sums = jnp.sum(jnp.transpose(sums), axis=0, keepdims=True)
    norm[...] = jnp.sqrt(sums / features + 1e-06) * math.sqrt(features)
    loop((multiply, 0))
    collect(0)
    loop((arrive, 2), (crossed, 1))
    loop((multiply, 1))
    collect(1)

    table = jnp.zeros((fan, rows), jnp.int32)
    for block in range(shards):
        table = table + jnp.where(owner[block] == me, routes[:, block * rows:(block + 1) * rows], 0)
    lanes = rows * fan
    flat = jnp.concatenate([table[j:j + 1] for j in range(fan)], axis=1)
    wide = jnp.broadcast_to(flat.astype(jnp.float32), (lanes, lanes))
    first_lane = lax.broadcasted_iota(jnp.int32, (lanes, lanes), 0)
    second_lane = lax.broadcasted_iota(jnp.int32, (lanes, lanes), 1)
    earlier = (jnp.transpose(wide) == wide) & (first_lane % rows < second_lane % rows)
    goal = flat * CAP + jnp.sum(earlier.astype(jnp.int32), axis=0, keepdims=True)
    moved = ((first_lane // rows == second_lane % fan) & (first_lane % rows == second_lane // fan)).astype(jnp.float32)
    goal = jnp.dot(jnp.broadcast_to(goal.astype(jnp.float32), (8, lanes)), moved,
                   precision=lax.Precision.HIGHEST, preferred_element_type=jnp.float32)[:1].astype(jnp.int32)
    pickup = (lax.broadcasted_iota(jnp.int32, (shards * CAP, lanes), 0) == goal).astype(jnp.float32)
    pickup = jnp.transpose(pickup)

    def second_last(part, carry):
        crossed(2, part)
        multiply(2, part)
        return carry

    def last(turn, carry):
        pl.when(turn < PARTS)(lambda: arrive(3, turn))
        pl.when((turn >= 1) & (turn <= PARTS))(lambda: crossed(3, turn - 1))
        pl.when(turn >= 2)(lambda: multiply(3, turn - 2))
        return carry

    lax.fori_loop(0, PARTS, second_last, 0)
    collect(2)
    lax.fori_loop(0, PARTS + 2, last, 0)
    collect(3)
    live = lax.broadcasted_iota(jnp.int32, (1, columns), 1) < counts[0]
    outgoing[...] = jnp.where(live, collected[...] / norm[...], 0.0).reshape(shards, CAP, columns)
    incoming[me] = outgoing[me]

    def score_copy(hop, peer):
        return remote(outgoing.at[peer], incoming.at[me], s_send.at[hop], s_recv.at[hop], peer)

    def send(hop, carry):
        score_copy(hop, (me + hop) % shards).start()
        return carry

    lax.fori_loop(1, shards, send, 0)

    def receive(hop, carry):
        source = (me + shards - hop) % shards
        remote(outgoing.at[source], incoming.at[source], s_send.at[hop], s_recv.at[hop], source).wait_recv()
        return carry

    lax.fori_loop(1, shards, receive, 0)
    out[...] = jnp.dot(pickup, incoming[...].reshape(shards * CAP, columns),
                       precision=lax.Precision.HIGHEST, preferred_element_type=jnp.float32)

    swap.wait_send()

    def finish(part, carry):
        for origin in range(LINE):
            y_copy(origin, part).wait_send()
            for kind in range(2):
                c_copy(kind, origin, part, core).wait_send()
        for step in range(LINE - 1):
            @pl.when((place >= step) & (place < LINE - 1))
            def _():
                z_copy(0, step, place - step, part, after).wait_send()

            @pl.when((place + step < LINE) & (place > 0))
            def _():
                z_copy(1, step, place + step, part, before).wait_send()
        return carry

    lax.fori_loop(0, PARTS, finish, 0)

    def sent(hop, carry):
        score_copy(hop, (me + hop) % shards).wait_send()
        return carry

    lax.fori_loop(1, shards, sent, 0)


def on_grid(query_grads, train_grads, precondition, routes, owner, counts):
    rows, features = query_grads.shape
    columns = train_grads.shape[0]
    fan = routes.shape[1]
    shards = 4 * LINE
    pair, extra = 2 * rows, 4 * CAP
    width = features // (2 * PARTS)
    vmem = pl.BlockSpec(memory_space=pltpu.VMEM)
    left = pl.BlockSpec(memory_space=pltpu.HBM)
    dma = pltpu.SemaphoreType.DMA
    out = pl.pallas_call(
        grid_kernel,
        out_shape=jax.ShapeDtypeStruct((rows * fan, columns), jnp.float32),
        in_specs=[left] * 6,
        out_specs=vmem,
        scratch_shapes=[
            pltpu.VMEM(routes.shape[::-1], jnp.int32),
            pltpu.SMEM(owner.shape, jnp.int32),
            pltpu.SMEM(counts.shape, jnp.int32),
            pltpu.VMEM((rows, features), jnp.bfloat16),
            pltpu.VMEM((features // 128, 128), jnp.float32),
            pltpu.VMEM((1, features), jnp.float32),
            pltpu.VMEM((2 * LINE, fan, pair), jnp.int32),
            pltpu.VMEM((2, PARTS, rows, width), jnp.bfloat16),
            pltpu.VMEM((PARTS, rows, width), jnp.bfloat16),
            pltpu.VMEM((LINE, 2 * PARTS, pair + extra, width), jnp.bfloat16),
            pltpu.VMEM((columns, features), jnp.bfloat16),
            pltpu.VMEM((1, columns), jnp.float32),
            pltpu.VMEM((LINE, PARTS, extra, width), jnp.bfloat16),
            pltpu.VMEM((LINE, extra, pair), jnp.bfloat16),
            pltpu.VMEM((LINE, shards * CAP, pair), jnp.float32),
            pltpu.VMEM((LINE, shards * CAP, extra), jnp.float32),
            pltpu.VMEM((LINE, pair + extra, columns), jnp.float32),
            pltpu.VMEM((shards * CAP, columns), jnp.float32),
            pltpu.VMEM((shards, CAP, columns), jnp.float32),
            pltpu.VMEM((shards, CAP, columns), jnp.float32),
            dma((2,)),
            dma((6,)),
            dma((2, LINE - 1, PARTS)),
            dma((LINE, PARTS)),
            dma((LINE, PARTS)),
            dma((LINE, PARTS)),
            dma((2, LINE, PARTS)),
            dma((2, LINE, PARTS)),
            dma((shards,)),
            dma((shards,)),
        ],
        compiler_params=pltpu.CompilerParams(
            collective_id=0, has_side_effects=True, vmem_limit_bytes=63 * 1024 * 1024),
    )(routes.T, owner, counts, query_grads, precondition.reshape(features // 128, 128), train_grads)
    return out.reshape(rows, fan, columns)


def solution(mesh):
    per_part = on_grid if mesh.shape["train"] == 4 * LINE else per_device
    return jax.shard_map(
        per_part,
        mesh=mesh,
        in_specs=(
            P(("groups", "train"), None),
            P(("groups", "train"), None),
            P("groups"),
            P("groups", None),
            P("groups"),
            P(("groups", "train")),
        ),
        out_specs=P(("groups", "train"), None, None),
        check_vma=False,
    )
```

```python
import math

import jax
import jax.numpy as jnp
from jax import lax
from jax.experimental import pallas as pl
from jax.experimental.pallas import tpu as pltpu
from jax.sharding import PartitionSpec as P

CAP = 8


def normalize(query_grads, precondition):
    scaled = query_grads.astype(jnp.float32) * precondition[None, :]
    spread = jnp.sqrt(jnp.mean(scaled * scaled, axis=1, keepdims=True) + 1e-06)
    return (scaled / spread).astype(jnp.bfloat16)


def slot_table(block_routes, shards):
    hit_table = jnp.sum(
        (block_routes[:, :, None] == jnp.arange(shards, dtype=jnp.int32)[None, None, :]).astype(
            jnp.int32
        ),
        axis=1,
        dtype=jnp.int32,
    )
    earlier = jnp.cumsum(hit_table, axis=0, dtype=jnp.int32) - hit_table
    return jnp.take_along_axis(earlier, block_routes, axis=1)


def fetch_home(result):
    return lax.all_to_all(result, "train", split_axis=0, concat_axis=0, tiled=True)


def per_device(query_grads, train_grads, precondition, routes, owner, counts):
    shards = lax.axis_size("train")
    position = lax.axis_index("train")
    block_size = query_grads.shape[0]
    features = train_grads.shape[1]
    capacity = CAP
    normed = normalize(query_grads, precondition)
    own_routes = lax.dynamic_slice_in_dim(routes, position * block_size, block_size, 0)
    target = own_routes * capacity + slot_table(own_routes, shards)
    lane_ids = jnp.arange(shards * capacity, dtype=jnp.int32)
    picked = jnp.any(target[:, :, None] == lane_ids[None, None, :], axis=1).astype(jnp.bfloat16)
    outgoing = lax.dot_general(
        picked, normed, (((0,), (0,)), ((), ())), preferred_element_type=jnp.float32
    )
    outgoing = outgoing.astype(jnp.bfloat16).reshape(shards, capacity, features)
    inverse = jnp.zeros((shards,), jnp.int32).at[owner].set(jnp.arange(shards, dtype=jnp.int32))
    row_norm = jnp.sqrt(jnp.mean(jnp.square(train_grads.astype(jnp.float32)), axis=1) + 1e-06)
    filled = jnp.arange(train_grads.shape[0], dtype=jnp.int32) < counts[0]
    arrived = lax.all_to_all(outgoing, "train", split_axis=0, concat_axis=0, tiled=True)
    flattened = arrived.reshape(-1, features)
    dotted = lax.dot_general(
        flattened, train_grads, (((1,), (1,)), ((), ())), preferred_element_type=jnp.float32
    )
    result = jnp.where(filled[None, :], dotted / (row_norm[None, :] * math.sqrt(features)), 0.0)
    result = result.reshape(arrived.shape[0], arrived.shape[1], -1)
    returned = fetch_home(result[inverse])
    owned_block = inverse[position]
    their_routes = lax.dynamic_slice_in_dim(routes, owned_block * block_size, block_size, 0)
    pickup = their_routes * capacity + slot_table(their_routes, shards)
    return returned.reshape(shards * capacity, -1)[pickup]


LINE = 4
PARTS = 2


def grid_kernel(routes_any, owner_any, counts_any, query_any, scale_any, train, out,
                routes, owner, counts, query, scale_tiles, scale, pairs_held,
                mine, other, held, train_vmem, norm, picked, select, table,
                results, collected, outgoing, incoming,
                raw_sem, load_sem, z_send, z_recv, y_send, y_recv, c_send, c_recv, s_send, s_recv):
    rows, features = query.shape
    fan = routes.shape[0]
    half = features // 2
    pair = 2 * rows
    total = held.shape[2]
    extra = total - pair
    width = held.shape[3]
    columns = train_vmem.shape[0]
    shards = 4 * LINE
    me = lax.axis_index("train")
    core = me % 2
    side = (me // 2) % 2
    place = me // 4
    mate = place * 4 + side * 2 + (1 - core)
    across = place * 4 + (1 - side) * 2 + core
    after, before = me + 4, me - 4

    loads = [pltpu.make_async_copy(source, target, load_sem.at[i]) for i, (source, target) in enumerate(
        [(query_any, query), (scale_any, scale_tiles), (routes_any, routes),
         (owner_any, owner), (counts_any, counts), (train, train_vmem)])]
    for load in loads:
        load.start()
    barrier = pltpu.get_barrier_semaphore()
    for hop in range(1, shards):
        pl.semaphore_signal(barrier, inc=1, device_id={"train": (me + hop) % shards},
                            device_id_type=pl.DeviceIdType.MESH)

    def remote(source, target, send, recv, device):
        return pltpu.make_async_remote_copy(
            src_ref=source, dst_ref=target, send_sem=send, recv_sem=recv,
            device_id={"train": device}, device_id_type=pl.DeviceIdType.MESH)

    def z_copy(direction, step, origin, part, device):
        block = held.at[origin, core * PARTS + part, pl.ds(0, pair)]
        return remote(block, block, z_send.at[direction, step, part], z_recv.at[origin, part], device)

    def y_copy(origin, part):
        block = held.at[origin, core * PARTS + part, pl.ds(pair, extra)]
        return remote(picked.at[origin, part], block, y_send.at[origin, part], y_recv.at[origin, part], across)

    def c_copy(kind, origin, part, lane):
        span = pl.ds(0, pair) if kind == 0 else pl.ds(pair, extra)
        block = held.at[origin, lane * PARTS + part, span]
        return remote(block, block, c_send.at[kind, origin, part], c_recv.at[kind, origin, part], mate)

    for load in loads[:2]:
        load.wait()
    for i in range(features // 128):
        scale[:, pl.ds(i * 128, 128)] = scale_tiles[i:i + 1, :]

    def squares(i, total_square):
        at = pl.ds(pl.multiple_of(i * width, width), width)
        value = query[:, at].astype(jnp.float32) * scale[:, at]
        return total_square + jnp.sum(value * value, axis=1, keepdims=True)

    square = lax.fori_loop(0, 2 * PARTS, squares, jnp.zeros((rows, 1), jnp.float32))
    spread = jnp.sqrt(square / features + 1e-06)

    def normalize_part(part, carry):
        for lane in range(2):
            at = pl.ds(pl.multiple_of(lane * half + part * width, width), width)
            value = query[:, at].astype(jnp.float32) * scale[:, at]
            mine[lane, part] = (value / spread).astype(jnp.bfloat16)
        return carry

    lax.fori_loop(0, PARTS, normalize_part, 0)
    pl.semaphore_wait(barrier, shards - 1)
    swap = remote(mine.at[1 - core], other, raw_sem.at[0], raw_sem.at[1], mate)
    swap.start()

    for load in loads[2:5]:
        load.wait()
    for i in range(2 * LINE):
        pairs_held[i] = routes[:, i * pair:(i + 1) * pair]
    lane = lax.broadcasted_iota(jnp.int32, (1, pair), 1)
    second_block = lane >= rows
    targets = [place * 4 + (1 - side) * 2, place * 4 + (1 - side) * 2 + 1, me]
    hits = []
    for origin in range(LINE):
        pairs = pairs_held[origin * 2 + side]
        for shard in targets:
            hits.append(jnp.sum((pairs == shard).astype(jnp.float32), axis=0, keepdims=True))
    hits = jnp.concatenate(hits + hits[:4], axis=0)
    first_lane = lax.broadcasted_iota(jnp.int32, (pair, pair), 0)
    second_lane = lax.broadcasted_iota(jnp.int32, (pair, pair), 1)
    earlier = ((first_lane < rows) == (second_lane < rows)) & (first_lane < second_lane)
    orders = jnp.dot(hits, earlier.astype(jnp.float32), preferred_element_type=jnp.float32).astype(jnp.int32)
    line = lax.broadcasted_iota(jnp.int32, (extra, pair), 0)
    for origin in range(LINE):
        chosen = None
        for core_there in range(2):
            at = origin * 3 + core_there
            goal = jnp.where(second_block, 2 * CAP, 0) + core_there * CAP + orders[at:at + 1]
            same = line == jnp.where(hits[at:at + 1] > 0.5, goal, -1)
            chosen = same if chosen is None else chosen | same
        select[origin] = chosen.astype(jnp.float32).astype(jnp.bfloat16)
    swap.wait_recv()

    def cross(origin, part):
        block = held[origin, core * PARTS + part, pl.ds(0, pair), :]
        chosen = jnp.dot(select[origin], block, preferred_element_type=jnp.float32)
        picked[origin, part] = chosen.astype(jnp.bfloat16)
        y_copy(origin, part).start()

    def first(part, carry):
        ours = mine[core, part].astype(jnp.float32)
        theirs = other[part].astype(jnp.float32)
        top = jnp.where(core == 0, ours, theirs)
        low = jnp.where(core == 0, theirs, ours)
        held[place, core * PARTS + part, pl.ds(0, pair), :] = jnp.concatenate([top, low], axis=0).astype(jnp.bfloat16)

        @pl.when(place < LINE - 1)
        def _():
            z_copy(0, 0, place, part, after).start()

        @pl.when(place > 0)
        def _():
            z_copy(1, 0, place, part, before).start()

        c_copy(0, place, part, core).start()
        cross(place, part)
        return carry

    lax.fori_loop(0, PARTS, first, 0)

    def sources(step):
        if step == 0:
            return [(None, place, None)]
        return [(place >= step, place - step, 0), (place + step < LINE, place + step, 1)]

    def under(condition, body):
        if condition is None:
            body()
        else:
            pl.when(condition)(body)

    def arrive(step, part):
        for condition, origin, direction in sources(step):
            def body(origin=origin, direction=direction):
                z_copy(direction, 0, origin, part, mate).wait_recv()
                if step < LINE - 1:
                    if direction == 0:
                        @pl.when(place < LINE - 1)
                        def _():
                            z_copy(0, step, origin, part, after).start()
                    else:
                        @pl.when(place > 0)
                        def _():
                            z_copy(1, step, origin, part, before).start()
                c_copy(0, origin, part, core).start()
                cross(origin, part)
            under(condition, body)

    def crossed(step, part):
        for condition, origin, _ in sources(step):
            def body(origin=origin):
                y_copy(origin, part).wait_recv()
                c_copy(1, origin, part, core).start()
            under(condition, body)

    def multiply(step, part):
        for condition, origin, _ in sources(step):
            def body(origin=origin):
                c_copy(0, origin, part, 1 - core).wait_recv()
                c_copy(1, origin, part, 1 - core).wait_recv()
                partial = jnp.zeros((total, columns), jnp.float32)
                for lane in range(2):
                    at = pl.ds(pl.multiple_of((lane * PARTS + part) * width, width), width)
                    partial = partial + lax.dot_general(
                        held[origin, lane * PARTS + part], train_vmem[:, at], (((1,), (1,)), ((), ())),
                        preferred_element_type=jnp.float32)
                results[origin] += partial
            under(condition, body)

    def loop(*work):
        def body(part, carry):
            for call, step in work:
                call(step, part)
            return carry
        lax.fori_loop(0, PARTS, body, 0)

    def collect(step):
        for condition, origin, _ in sources(step):
            def body(origin=origin):
                collected[...] += jnp.dot(
                    table[origin], results[origin],
                    precision=lax.Precision.HIGHEST, preferred_element_type=jnp.float32)
            under(condition, body)

    results[...] = jnp.zeros_like(results)
    collected[...] = jnp.zeros_like(collected)

    far_lane = lax.broadcasted_iota(jnp.int32, (1, extra), 1)
    far_second = far_lane >= 2 * CAP
    far_slot = far_lane - jnp.where(far_second, 2 * CAP, 0) - core * CAP
    far_valid = (far_slot >= 0) & (far_slot < CAP)
    tall = lax.broadcasted_iota(jnp.int32, (shards * CAP, total), 0)
    for origin in range(LINE):
        at = origin * 3 + 2
        near = (origin * 2 + side) * 2
        home = jnp.where(second_block, owner[near + 1], owner[near])
        near_goal = jnp.where(hits[at:at + 1] > 0.5, home * CAP + orders[at:at + 1], -1)
        far = (origin * 2 + 1 - side) * 2
        home = jnp.where(far_second, owner[far + 1], owner[far])
        far_goal = jnp.where(far_valid, home * CAP + far_slot, -1)
        table[origin] = (tall == jnp.concatenate([near_goal, far_goal], axis=1)).astype(jnp.float32)

    loop((arrive, 1), (crossed, 0))
    loads[5].wait()

    def train_squares(i, sums):
        at = pl.ds(pl.multiple_of(i * 512, 512), 512)
        value = train_vmem[:, at].astype(jnp.float32)
        value = value * value
        return sums + (value[:, :128] + value[:, 128:256]) + (value[:, 256:384] + value[:, 384:])

    sums = lax.fori_loop(0, features // 512, train_squares, jnp.zeros((columns, 128), jnp.float32))
    sums = jnp.sum(jnp.transpose(sums), axis=0, keepdims=True)
    norm[...] = jnp.sqrt(sums / features + 1e-06) * math.sqrt(features)
    loop((multiply, 0))
    arrive(2, 0)
    crossed(1, 0)
    collect(0)
    multiply(1, 0)
    arrive(2, 1)
    crossed(1, 1)
    multiply(1, 1)
    collect(1)

    named = jnp.zeros((fan, rows), jnp.int32)
    for block in range(shards):
        named = named + jnp.where(owner[block] == me, routes[:, block * rows:(block + 1) * rows], 0)
    lanes = rows * fan
    flat = jnp.concatenate([named[j:j + 1] for j in range(fan)], axis=1)
    wide = jnp.broadcast_to(flat.astype(jnp.float32), (lanes, lanes))
    first_lane = lax.broadcasted_iota(jnp.int32, (lanes, lanes), 0)
    second_lane = lax.broadcasted_iota(jnp.int32, (lanes, lanes), 1)
    first_query = first_lane - rows * sum((first_lane >= rows * j).astype(jnp.int32) for j in range(1, fan))
    second_query = second_lane - rows * sum((second_lane >= rows * j).astype(jnp.int32) for j in range(1, fan))
    earlier = (jnp.transpose(wide) == wide) & (first_query < second_query)
    goal = flat * CAP + jnp.sum(earlier.astype(jnp.int32), axis=0, keepdims=True)
    moved = ((first_lane - first_query) + first_query * (rows * fan) == (second_lane % fan) * rows + (second_lane // fan) * (rows * fan)).astype(jnp.float32)
    goal = jnp.dot(jnp.broadcast_to(goal.astype(jnp.float32), (8, lanes)), moved,
                   precision=lax.Precision.HIGHEST, preferred_element_type=jnp.float32)[:1].astype(jnp.int32)
    pickup = (lax.broadcasted_iota(jnp.int32, (shards * CAP, lanes), 0) == goal).astype(jnp.float32)
    pickup = jnp.transpose(pickup)

    arrive(3, 0)
    loop((crossed, 2), (multiply, 2))
    collect(2)
    crossed(3, 0)
    arrive(3, 1)
    multiply(3, 0)
    crossed(3, 1)
    multiply(3, 1)
    collect(3)
    live = lax.broadcasted_iota(jnp.int32, (1, columns), 1) < counts[0]
    outgoing[...] = jnp.where(live, collected[...] / norm[...], 0.0).reshape(shards, CAP, columns)
    incoming[me] = outgoing[me]

    def score_copy(hop, peer):
        return remote(outgoing.at[peer], incoming.at[me], s_send.at[hop], s_recv.at[hop], peer)

    def send(hop, carry):
        score_copy(hop, (me + hop) % shards).start()
        return carry

    lax.fori_loop(1, shards, send, 0)

    def receive(hop, carry):
        source = (me + shards - hop) % shards
        remote(outgoing.at[source], incoming.at[source], s_send.at[hop], s_recv.at[hop], source).wait_recv()
        return carry

    lax.fori_loop(1, shards, receive, 0)
    out[...] = jnp.dot(pickup, incoming[...].reshape(shards * CAP, columns),
                       precision=lax.Precision.HIGHEST, preferred_element_type=jnp.float32)

    swap.wait_send()

    def finish(part, carry):
        for origin in range(LINE):
            y_copy(origin, part).wait_send()
            for kind in range(2):
                c_copy(kind, origin, part, core).wait_send()
        for step in range(LINE - 1):
            @pl.when((place >= step) & (place < LINE - 1))
            def _():
                z_copy(0, step, place - step, part, after).wait_send()

            @pl.when((place + step < LINE) & (place > 0))
            def _():
                z_copy(1, step, place + step, part, before).wait_send()
        return carry

    lax.fori_loop(0, PARTS, finish, 0)

    def sent(hop, carry):
        score_copy(hop, (me + hop) % shards).wait_send()
        return carry

    lax.fori_loop(1, shards, sent, 0)


def on_grid(query_grads, train_grads, precondition, routes, owner, counts):
    rows, features = query_grads.shape
    columns = train_grads.shape[0]
    fan = routes.shape[1]
    shards = 4 * LINE
    pair, extra = 2 * rows, 4 * CAP
    width = features // (2 * PARTS)
    vmem = pl.BlockSpec(memory_space=pltpu.VMEM)
    left = pl.BlockSpec(memory_space=pltpu.HBM)
    dma = pltpu.SemaphoreType.DMA
    out = pl.pallas_call(
        grid_kernel,
        out_shape=jax.ShapeDtypeStruct((rows * fan, columns), jnp.float32),
        in_specs=[left] * 6,
        out_specs=vmem,
        scratch_shapes=[
            pltpu.VMEM(routes.shape[::-1], jnp.int32),
            pltpu.SMEM(owner.shape, jnp.int32),
            pltpu.SMEM(counts.shape, jnp.int32),
            pltpu.VMEM((rows, features), jnp.bfloat16),
            pltpu.VMEM((features // 128, 128), jnp.float32),
            pltpu.VMEM((1, features), jnp.float32),
            pltpu.VMEM((2 * LINE, fan, pair), jnp.int32),
            pltpu.VMEM((2, PARTS, rows, width), jnp.bfloat16),
            pltpu.VMEM((PARTS, rows, width), jnp.bfloat16),
            pltpu.VMEM((LINE, 2 * PARTS, pair + extra, width), jnp.bfloat16),
            pltpu.VMEM((columns, features), jnp.bfloat16),
            pltpu.VMEM((1, columns), jnp.float32),
            pltpu.VMEM((LINE, PARTS, extra, width), jnp.bfloat16),
            pltpu.VMEM((LINE, extra, pair), jnp.bfloat16),
            pltpu.VMEM((LINE, shards * CAP, pair + extra), jnp.float32),
            pltpu.VMEM((LINE, pair + extra, columns), jnp.float32),
            pltpu.VMEM((shards * CAP, columns), jnp.float32),
            pltpu.VMEM((shards, CAP, columns), jnp.float32),
            pltpu.VMEM((shards, CAP, columns), jnp.float32),
            dma((2,)),
            dma((6,)),
            dma((2, LINE - 1, PARTS)),
            dma((LINE, PARTS)),
            dma((LINE, PARTS)),
            dma((LINE, PARTS)),
            dma((2, LINE, PARTS)),
            dma((2, LINE, PARTS)),
            dma((shards,)),
            dma((shards,)),
        ],
        compiler_params=pltpu.CompilerParams(
            collective_id=0, has_side_effects=True, vmem_limit_bytes=63 * 1024 * 1024),
    )(routes.T, owner, counts, query_grads, precondition.reshape(features // 128, 128), train_grads)
    return out.reshape(rows, fan, columns)


def solution(mesh):
    per_part = on_grid if mesh.shape["train"] == 4 * LINE else per_device
    return jax.shard_map(
        per_part,
        mesh=mesh,
        in_specs=(
            P(("groups", "train"), None),
            P(("groups", "train"), None),
            P("groups"),
            P("groups", None),
            P("groups"),
            P(("groups", "train")),
        ),
        out_specs=P(("groups", "train"), None, None),
        check_vma=False,
    )
```

```python
import math

import jax
import jax.numpy as jnp
from jax import lax
from jax.experimental import pallas as pl
from jax.experimental.pallas import tpu as pltpu
from jax.sharding import PartitionSpec as P

CAP = 8


def normalize(query_grads, precondition):
    scaled = query_grads.astype(jnp.float32) * precondition[None, :]
    spread = jnp.sqrt(jnp.mean(scaled * scaled, axis=1, keepdims=True) + 1e-06)
    return (scaled / spread).astype(jnp.bfloat16)


def slot_table(block_routes, shards):
    hit_table = jnp.sum(
        (block_routes[:, :, None] == jnp.arange(shards, dtype=jnp.int32)[None, None, :]).astype(
            jnp.int32
        ),
        axis=1,
        dtype=jnp.int32,
    )
    earlier = jnp.cumsum(hit_table, axis=0, dtype=jnp.int32) - hit_table
    return jnp.take_along_axis(earlier, block_routes, axis=1)


def fetch_home(result):
    return lax.all_to_all(result, "train", split_axis=0, concat_axis=0, tiled=True)


def per_device(query_grads, train_grads, precondition, routes, owner, counts):
    shards = lax.axis_size("train")
    position = lax.axis_index("train")
    block_size = query_grads.shape[0]
    features = train_grads.shape[1]
    capacity = CAP
    normed = normalize(query_grads, precondition)
    own_routes = lax.dynamic_slice_in_dim(routes, position * block_size, block_size, 0)
    target = own_routes * capacity + slot_table(own_routes, shards)
    lane_ids = jnp.arange(shards * capacity, dtype=jnp.int32)
    picked = jnp.any(target[:, :, None] == lane_ids[None, None, :], axis=1).astype(jnp.bfloat16)
    outgoing = lax.dot_general(
        picked, normed, (((0,), (0,)), ((), ())), preferred_element_type=jnp.float32
    )
    outgoing = outgoing.astype(jnp.bfloat16).reshape(shards, capacity, features)
    inverse = jnp.zeros((shards,), jnp.int32).at[owner].set(jnp.arange(shards, dtype=jnp.int32))
    row_norm = jnp.sqrt(jnp.mean(jnp.square(train_grads.astype(jnp.float32)), axis=1) + 1e-06)
    filled = jnp.arange(train_grads.shape[0], dtype=jnp.int32) < counts[0]
    arrived = lax.all_to_all(outgoing, "train", split_axis=0, concat_axis=0, tiled=True)
    flattened = arrived.reshape(-1, features)
    dotted = lax.dot_general(
        flattened, train_grads, (((1,), (1,)), ((), ())), preferred_element_type=jnp.float32
    )
    result = jnp.where(filled[None, :], dotted / (row_norm[None, :] * math.sqrt(features)), 0.0)
    result = result.reshape(arrived.shape[0], arrived.shape[1], -1)
    returned = fetch_home(result[inverse])
    owned_block = inverse[position]
    their_routes = lax.dynamic_slice_in_dim(routes, owned_block * block_size, block_size, 0)
    pickup = their_routes * capacity + slot_table(their_routes, shards)
    return returned.reshape(shards * capacity, -1)[pickup]


LINE = 4
PARTS = 2


def grid_kernel(routes_any, owner_any, counts_any, query_any, scale_any, train, out,
                routes, owner, counts, query, scale_tiles, scale, pairs_held,
                mine, other, held, train_vmem, norm, picked, select, table,
                results, collected, outgoing, incoming,
                raw_sem, load_sem, z_send, z_recv, y_send, y_recv, c_send, c_recv, s_send, s_recv):
    rows, features = query.shape
    fan = routes.shape[0]
    half = features // 2
    pair = 2 * rows
    total = held.shape[2]
    extra = total - pair
    width = held.shape[3]
    columns = train_vmem.shape[0]
    shards = 4 * LINE
    me = lax.axis_index("train")
    core = me % 2
    side = (me // 2) % 2
    place = me // 4
    mate = place * 4 + side * 2 + (1 - core)
    across = place * 4 + (1 - side) * 2 + core
    after, before = me + 4, me - 4

    loads = [pltpu.make_async_copy(source, target, load_sem.at[i]) for i, (source, target) in enumerate(
        [(query_any, query), (scale_any, scale_tiles), (routes_any, routes),
         (owner_any, owner), (counts_any, counts), (train, train_vmem)])]
    for load in loads:
        load.start()
    barrier = pltpu.get_barrier_semaphore()
    for hop in range(1, shards):
        pl.semaphore_signal(barrier, inc=1, device_id={"train": (me + hop) % shards},
                            device_id_type=pl.DeviceIdType.MESH)

    def remote(source, target, send, recv, device):
        return pltpu.make_async_remote_copy(
            src_ref=source, dst_ref=target, send_sem=send, recv_sem=recv,
            device_id={"train": device}, device_id_type=pl.DeviceIdType.MESH)

    def z_copy(direction, step, origin, part, device):
        block = held.at[origin, core * PARTS + part, pl.ds(0, pair)]
        return remote(block, block, z_send.at[direction, step, part], z_recv.at[origin, part], device)

    def y_copy(origin, part):
        block = held.at[origin, core * PARTS + part, pl.ds(pair, extra)]
        return remote(picked.at[origin, part], block, y_send.at[origin, part], y_recv.at[origin, part], across)

    def c_copy(kind, origin, part, lane):
        span = pl.ds(0, pair) if kind == 0 else pl.ds(pair, extra)
        block = held.at[origin, lane * PARTS + part, span]
        return remote(block, block, c_send.at[kind, origin, part], c_recv.at[kind, origin, part], mate)

    for load in loads[:2]:
        load.wait()
    for i in range(features // 128):
        scale[:, pl.ds(i * 128, 128)] = scale_tiles[i:i + 1, :]

    def squares(i, total_square):
        at = pl.ds(pl.multiple_of(i * width, width), width)
        value = query[:, at].astype(jnp.float32) * scale[:, at]
        return total_square + jnp.sum(value * value, axis=1, keepdims=True)

    square = lax.fori_loop(0, 2 * PARTS, squares, jnp.zeros((rows, 1), jnp.float32))
    spread = 1.0 / jnp.sqrt(square / features + 1e-06)

    def normalize_part(part, carry):
        for lane in range(2):
            at = pl.ds(pl.multiple_of(lane * half + part * width, width), width)
            value = query[:, at].astype(jnp.float32) * scale[:, at]
            mine[lane, part] = (value * spread).astype(jnp.bfloat16)
        return carry

    lax.fori_loop(0, PARTS, normalize_part, 0)
    pl.semaphore_wait(barrier, shards - 1)
    swap = remote(mine.at[1 - core], other, raw_sem.at[0], raw_sem.at[1], mate)
    swap.start()

    for load in loads[2:5]:
        load.wait()
    for i in range(2 * LINE):
        pairs_held[i] = routes[:, i * pair:(i + 1) * pair]
    lane = lax.broadcasted_iota(jnp.int32, (1, pair), 1)
    second_block = lane >= rows
    targets = [place * 4 + (1 - side) * 2, place * 4 + (1 - side) * 2 + 1, me]
    hits = []
    for origin in range(LINE):
        pairs = pairs_held[origin * 2 + side]
        for shard in targets:
            hits.append(jnp.sum((pairs == shard).astype(jnp.float32), axis=0, keepdims=True))
    hits = jnp.concatenate(hits + hits[:4], axis=0)
    first_lane = lax.broadcasted_iota(jnp.int32, (pair, pair), 0)
    second_lane = lax.broadcasted_iota(jnp.int32, (pair, pair), 1)
    earlier = ((first_lane < rows) == (second_lane < rows)) & (first_lane < second_lane)
    orders = jnp.dot(hits, earlier.astype(jnp.float32), preferred_element_type=jnp.float32).astype(jnp.int32)
    line = lax.broadcasted_iota(jnp.int32, (extra, pair), 0)
    for origin in range(LINE):
        chosen = None
        for core_there in range(2):
            at = origin * 3 + core_there
            goal = jnp.where(second_block, 2 * CAP, 0) + core_there * CAP + orders[at:at + 1]
            same = line == jnp.where(hits[at:at + 1] > 0.5, goal, -1)
            chosen = same if chosen is None else chosen | same
        select[origin] = chosen.astype(jnp.float32).astype(jnp.bfloat16)
    swap.wait_recv()

    def cross(origin, part):
        block = held[origin, core * PARTS + part, pl.ds(0, pair), :]
        chosen = jnp.dot(select[origin], block, preferred_element_type=jnp.float32)
        picked[origin, part] = chosen.astype(jnp.bfloat16)
        y_copy(origin, part).start()

    def first(part, carry):
        ours = mine[core, part].astype(jnp.float32)
        theirs = other[part].astype(jnp.float32)
        top = jnp.where(core == 0, ours, theirs)
        low = jnp.where(core == 0, theirs, ours)
        held[place, core * PARTS + part, pl.ds(0, pair), :] = jnp.concatenate([top, low], axis=0).astype(jnp.bfloat16)

        @pl.when(place < LINE - 1)
        def _():
            z_copy(0, 0, place, part, after).start()

        @pl.when(place > 0)
        def _():
            z_copy(1, 0, place, part, before).start()

        c_copy(0, place, part, core).start()
        return carry

    lax.fori_loop(0, PARTS, first, 0)
    for part in range(PARTS):
        cross(place, part)

    def sources(step):
        if step == 0:
            return [(None, place, None)]
        return [(place >= step, place - step, 0), (place + step < LINE, place + step, 1)]

    def under(condition, body):
        if condition is None:
            body()
        else:
            pl.when(condition)(body)

    def arrive(step, part):
        for condition, origin, direction in sources(step):
            def body(origin=origin, direction=direction):
                z_copy(direction, 0, origin, part, mate).wait_recv()
                if step < LINE - 1:
                    if direction == 0:
                        @pl.when(place < LINE - 1)
                        def _():
                            z_copy(0, step, origin, part, after).start()
                    else:
                        @pl.when(place > 0)
                        def _():
                            z_copy(1, step, origin, part, before).start()
                c_copy(0, origin, part, core).start()
            under(condition, body)
        for condition, origin, direction in sources(step):
            def body(origin=origin):
                cross(origin, part)
            under(condition, body)

    def crossed(step, part):
        for condition, origin, _ in sources(step):
            def body(origin=origin):
                y_copy(origin, part).wait_recv()
                c_copy(1, origin, part, core).start()
            under(condition, body)

    def multiply(step, part):
        for condition, origin, _ in sources(step):
            def body(origin=origin):
                c_copy(0, origin, part, 1 - core).wait_recv()
                c_copy(1, origin, part, 1 - core).wait_recv()
                partial = jnp.zeros((total, columns), jnp.float32)
                for lane in range(2):
                    at = pl.ds(pl.multiple_of((lane * PARTS + part) * width, width), width)
                    partial = partial + lax.dot_general(
                        held[origin, lane * PARTS + part], train_vmem[:, at], (((1,), (1,)), ((), ())),
                        preferred_element_type=jnp.float32)
                results[origin] += partial
            under(condition, body)

    def loop(*work):
        def body(part, carry):
            for call, step in work:
                call(step, part)
            return carry
        lax.fori_loop(0, PARTS, body, 0)

    def collect(step):
        for condition, origin, _ in sources(step):
            def body(origin=origin):
                collected[...] += jnp.dot(
                    table[origin], results[origin],
                    precision=lax.Precision.HIGHEST, preferred_element_type=jnp.float32)
            under(condition, body)

    results[...] = jnp.zeros_like(results)
    collected[...] = jnp.zeros_like(collected)

    far_lane = lax.broadcasted_iota(jnp.int32, (1, extra), 1)
    far_second = far_lane >= 2 * CAP
    far_slot = far_lane - jnp.where(far_second, 2 * CAP, 0) - core * CAP
    far_valid = (far_slot >= 0) & (far_slot < CAP)
    tall = lax.broadcasted_iota(jnp.int32, (shards * CAP, total), 0)
    for origin in range(LINE):
        at = origin * 3 + 2
        near = (origin * 2 + side) * 2
        home = jnp.where(second_block, owner[near + 1], owner[near])
        near_goal = jnp.where(hits[at:at + 1] > 0.5, home * CAP + orders[at:at + 1], -1)
        far = (origin * 2 + 1 - side) * 2
        home = jnp.where(far_second, owner[far + 1], owner[far])
        far_goal = jnp.where(far_valid, home * CAP + far_slot, -1)
        table[origin] = (tall == jnp.concatenate([near_goal, far_goal], axis=1)).astype(jnp.float32)

    loop((arrive, 1), (crossed, 0))
    loads[5].wait()

    def train_squares(i, sums):
        at = pl.ds(pl.multiple_of(i * 512, 512), 512)
        value = train_vmem[:, at].astype(jnp.float32)
        value = value * value
        return sums + (value[:, :128] + value[:, 128:256]) + (value[:, 256:384] + value[:, 384:])

    sums = lax.fori_loop(0, features // 512, train_squares, jnp.zeros((columns, 128), jnp.float32))
    sums = jnp.sum(jnp.transpose(sums), axis=0, keepdims=True)
    norm[...] = jnp.sqrt(sums / features + 1e-06) * math.sqrt(features)
    loop((multiply, 0))
    arrive(2, 0)
    crossed(1, 0)
    collect(0)
    multiply(1, 0)
    arrive(2, 1)
    crossed(1, 1)
    multiply(1, 1)
    collect(1)

    named = jnp.zeros((fan, rows), jnp.int32)
    for block in range(shards):
        named = named + jnp.where(owner[block] == me, routes[:, block * rows:(block + 1) * rows], 0)
    lanes = rows * fan
    flat = jnp.concatenate([named[j:j + 1] for j in range(fan)], axis=1)
    wide = jnp.broadcast_to(flat.astype(jnp.float32), (lanes, lanes))
    first_lane = lax.broadcasted_iota(jnp.int32, (lanes, lanes), 0)
    second_lane = lax.broadcasted_iota(jnp.int32, (lanes, lanes), 1)
    first_query = first_lane - rows * sum((first_lane >= rows * j).astype(jnp.int32) for j in range(1, fan))
    second_query = second_lane - rows * sum((second_lane >= rows * j).astype(jnp.int32) for j in range(1, fan))
    earlier = (jnp.transpose(wide) == wide) & (first_query < second_query)
    goal = flat * CAP + jnp.sum(earlier.astype(jnp.int32), axis=0, keepdims=True)
    moved = ((first_lane - first_query) + first_query * (rows * fan) == (second_lane % fan) * rows + (second_lane // fan) * (rows * fan)).astype(jnp.float32)
    goal = jnp.dot(jnp.broadcast_to(goal.astype(jnp.float32), (8, lanes)), moved,
                   precision=lax.Precision.HIGHEST, preferred_element_type=jnp.float32)[:1].astype(jnp.int32)
    pickup = (lax.broadcasted_iota(jnp.int32, (shards * CAP, lanes), 0) == goal).astype(jnp.float32)
    pickup = jnp.transpose(pickup)

    arrive(3, 0)
    loop((crossed, 2), (multiply, 2))
    collect(2)
    crossed(3, 0)
    arrive(3, 1)
    multiply(3, 0)
    crossed(3, 1)
    multiply(3, 1)
    collect(3)
    live = lax.broadcasted_iota(jnp.int32, (1, columns), 1) < counts[0]
    outgoing[...] = jnp.where(live, collected[...] / norm[...], 0.0).reshape(shards, CAP, columns)
    incoming[me] = outgoing[me]

    def score_copy(hop, peer):
        return remote(outgoing.at[peer], incoming.at[me], s_send.at[hop], s_recv.at[hop], peer)

    def send(hop, carry):
        score_copy(hop, (me + hop) % shards).start()
        return carry

    lax.fori_loop(1, shards, send, 0)

    def receive(hop, carry):
        source = (me + shards - hop) % shards
        remote(outgoing.at[source], incoming.at[source], s_send.at[hop], s_recv.at[hop], source).wait_recv()
        return carry

    lax.fori_loop(1, shards, receive, 0)
    out[...] = jnp.dot(pickup, incoming[...].reshape(shards * CAP, columns),
                       precision=lax.Precision.HIGHEST, preferred_element_type=jnp.float32)

    swap.wait_send()

    def finish(part, carry):
        for origin in range(LINE):
            y_copy(origin, part).wait_send()
            for kind in range(2):
                c_copy(kind, origin, part, core).wait_send()
        for step in range(LINE - 1):
            @pl.when((place >= step) & (place < LINE - 1))
            def _():
                z_copy(0, step, place - step, part, after).wait_send()

            @pl.when((place + step < LINE) & (place > 0))
            def _():
                z_copy(1, step, place + step, part, before).wait_send()
        return carry

    lax.fori_loop(0, PARTS, finish, 0)

    def sent(hop, carry):
        score_copy(hop, (me + hop) % shards).wait_send()
        return carry

    lax.fori_loop(1, shards, sent, 0)


def on_grid(query_grads, train_grads, precondition, routes, owner, counts):
    rows, features = query_grads.shape
    columns = train_grads.shape[0]
    fan = routes.shape[1]
    shards = 4 * LINE
    pair, extra = 2 * rows, 4 * CAP
    width = features // (2 * PARTS)
    vmem = pl.BlockSpec(memory_space=pltpu.VMEM)
    left = pl.BlockSpec(memory_space=pltpu.HBM)
    dma = pltpu.SemaphoreType.DMA
    out = pl.pallas_call(
        grid_kernel,
        out_shape=jax.ShapeDtypeStruct((rows * fan, columns), jnp.float32),
        in_specs=[left] * 6,
        out_specs=vmem,
        scratch_shapes=[
            pltpu.VMEM(routes.shape[::-1], jnp.int32),
            pltpu.SMEM(owner.shape, jnp.int32),
            pltpu.SMEM(counts.shape, jnp.int32),
            pltpu.VMEM((rows, features), jnp.bfloat16),
            pltpu.VMEM((features // 128, 128), jnp.float32),
            pltpu.VMEM((1, features), jnp.float32),
            pltpu.VMEM((2 * LINE, fan, pair), jnp.int32),
            pltpu.VMEM((2, PARTS, rows, width), jnp.bfloat16),
            pltpu.VMEM((PARTS, rows, width), jnp.bfloat16),
            pltpu.VMEM((LINE, 2 * PARTS, pair + extra, width), jnp.bfloat16),
            pltpu.VMEM((columns, features), jnp.bfloat16),
            pltpu.VMEM((1, columns), jnp.float32),
            pltpu.VMEM((LINE, PARTS, extra, width), jnp.bfloat16),
            pltpu.VMEM((LINE, extra, pair), jnp.bfloat16),
            pltpu.VMEM((LINE, shards * CAP, pair + extra), jnp.float32),
            pltpu.VMEM((LINE, pair + extra, columns), jnp.float32),
            pltpu.VMEM((shards * CAP, columns), jnp.float32),
            pltpu.VMEM((shards, CAP, columns), jnp.float32),
            pltpu.VMEM((shards, CAP, columns), jnp.float32),
            dma((2,)),
            dma((6,)),
            dma((2, LINE - 1, PARTS)),
            dma((LINE, PARTS)),
            dma((LINE, PARTS)),
            dma((LINE, PARTS)),
            dma((2, LINE, PARTS)),
            dma((2, LINE, PARTS)),
            dma((shards,)),
            dma((shards,)),
        ],
        compiler_params=pltpu.CompilerParams(
            collective_id=0, has_side_effects=True, vmem_limit_bytes=63 * 1024 * 1024),
    )(routes.T, owner, counts, query_grads, precondition.reshape(features // 128, 128), train_grads)
    return out.reshape(rows, fan, columns)


def solution(mesh):
    per_part = on_grid if mesh.shape["train"] == 4 * LINE else per_device
    return jax.shard_map(
        per_part,
        mesh=mesh,
        in_specs=(
            P(("groups", "train"), None),
            P(("groups", "train"), None),
            P("groups"),
            P("groups", None),
            P("groups"),
            P(("groups", "train")),
        ),
        out_specs=P(("groups", "train"), None, None),
        check_vma=False,
    )
```
